32 devices in a mesh: grp: 2 (over y), blk: 4 (over x, core), hid: 4 (over z).
Axes of the slice: x: 2, y: 2, z: 4, core: 2. Of those that a mesh axis runs over, the one named last changes fastest.
Arguments:
- tokens: bfloat16 [1024, 4096], P(('grp', 'blk'), 'hid'), parts along dimension 0, may hold values from -6 to 6
- grad_out: bfloat16 [1024, 4096], P(('grp', 'blk'), 'hid'), parts along dimension 0, may hold values from -0.59765625 to 0.59765625
- expert_ids: int32 [1024, 8], P(('grp', 'blk')), parts along dimension 0, may hold values from 0 to 15, all different within a row; in each aligned block of 128 rows (0 to 127, 128 to 255, ...) at most 68 rows name the same one
- route_probs: float32 [1024, 8], P(('grp', 'blk')), parts along dimension 0, may hold values from 0.1 to 1
- gate_w: bfloat16 [16, 4096, 1536], P('blk', None, 'hid'), may hold values from -0.09375 to 0.09375
- up_w: bfloat16 [16, 4096, 1536], P('blk', None, 'hid'), may hold values from -0.09375 to 0.09375
- down_w: bfloat16 [16, 1536, 4096], P('blk', 'hid'), may hold values from -0.15625 to 0.15625
Outputs:
- grad_tokens: bfloat16 [1024, 4096], P(('grp', 'blk'), 'hid'), parts along dimension 0
- grad_gate: bfloat16 [32, 4096, 1536], P(('grp', 'blk'), None, 'hid'), parts along dimension 0
- grad_up: bfloat16 [32, 4096, 1536], P(('grp', 'blk'), None, 'hid'), parts along dimension 0
- grad_down: bfloat16 [32, 1536, 4096], P(('grp', 'blk'), 'hid'), parts along dimension 0
The draws below stay inside these ranges and needn't reach their ends.
There are 2 independent parts, one for each index of `grp`. The reference program is written for one: setup_inputs(seed, part) draws one part's arguments, and reference() takes and returns one part's arrays. A program takes and returns all parts, laid end to end along the dimension named above; an argument that names none is the same for every part. Nothing has to cross between parts.
Inputs may be any that keep to these rules, and one draw needn't show every extreme that they name: `expert_ids`: in the rows of one token group (128 tokens, aligned blocks) each token names 8 different experts, and no expert is named by more than 68 tokens of the group; some expert is named by exactly 68.
All inputs are finite; a program needn't handle non-finite values.
Results may differ from the reference program's by a relative error of at most 0.012.
Values may be sent and summed in bfloat16 or wider, within the bound.
A program may use at most 256 MiB of HBM per device.

```python
import math
import jax
import jax.numpy as jnp
import numpy as np
from jax import lax

D = 4096
FF = 1536
TOP = 8
EXPERTS = 16
TOK_DEV = 128
CAP = 68
TOKENS = 512
N_BLK = 4
N_HID = 4


def level_of(key, extent, split, smallest, top_value):
    loudness = 1.0
    for position, blocks in split:
        steps = jax.random.uniform(jax.random.fold_in(jax.random.fold_in(key, 6), position), (blocks,), jnp.float32, smallest / len(split), top_value / len(split))
        loudness = loudness * jnp.repeat(jnp.exp(steps), extent[position] // blocks).reshape((-1,) + (1,) * (len(extent) - 1 - position))
    return loudness


def shared_out(rng, own, number, rows, amount, top, limit, skew):
    order = jax.random.permutation(rng, amount)
    heavy_load, ordinary = portions_of(amount, rows * top, limit, skew, True), portions_of(amount, rows * top, limit, skew, False)
    places = jnp.arange(amount)

    def named(tallies, rotation):
        used = int((tallies > 0).sum())
        fixed = max(1, used // 4)
        moved = fixed + (places - fixed + rotation * (used - fixed)) % max(1, amount - fixed)
        return jnp.zeros((amount,), jnp.int32).at[order[jnp.where(places < fixed, places, moved)]].set(jnp.asarray(tallies, jnp.int32))

    tallies = jnp.where(number % 4 == 0, named(heavy_load, number // 4), named(ordinary, number - number // 4 - 1))
    mixed = jax.random.permutation(jax.random.fold_in(own, 3), amount)
    donor, receiver = mixed[0:amount // 2 * 2:2], mixed[1:amount // 2 * 2:2]
    room = jnp.minimum(tallies[donor] - 1, limit - tallies[receiver]) // 2
    room = jnp.where((donor == order[0]) | (receiver == order[0]) | (tallies[receiver] == 0), 0, jnp.maximum(room, 0))
    moved = jax.random.randint(jax.random.fold_in(own, 4), (amount // 2,), 0, 1 << 20) % (room + 1)
    tallies = tallies.at[donor].add(-moved).at[receiver].add(moved)
    members = jnp.searchsorted(jnp.cumsum(tallies), jnp.arange(rows * top), side="right").astype(jnp.int32)
    grid = members.reshape(top, rows).T
    grid = grid[jax.random.permutation(jax.random.fold_in(own, 1), rows)]
    rotation = jax.random.randint(jax.random.fold_in(own, 2), (rows, 1), 0, top)
    return jnp.take_along_axis(grid, (jnp.arange(top)[None, :] + rotation) % top, axis=1)


def portions_of(count, total, bound, slope, full):
    weights = [(1 << 20) // math.isqrt(grade ** slope) + 1 for grade in range(1, count + 1)]
    largest = bound if full else min(bound, max(-(-total // count), total * weights[0] // sum(weights)))
    least = 1 if total - largest >= count - 1 else 0
    counts, surplus = [largest] + [least] * (count - 1), total - largest - least * (count - 1)
    while surplus > 0:
        free = [i for i in range(1, count) if counts[i] < largest] or [i for i in range(1, count) if counts[i] < bound]
        mass, budget = sum([weights[i] for i in free]), surplus
        for i in free:
            addition = min(bound - counts[i], max(1, budget * weights[i] // mass), surplus)
            counts[i] = counts[i] + addition
            surplus = surplus - addition
    return np.array(counts)


def scatter_about(stream_key, extent, scale, reach, pieces=(), held_as=jnp.bfloat16):
    array = scale * jax.random.normal(stream_key, extent, jnp.float32)
    if pieces:
        array = array * level_of(stream_key, extent, pieces, -0.22, 0.18)
    return jnp.clip(array, -reach, reach).astype(held_as)


def setup_inputs(seed: int = 0, part: int = 0) -> dict:
    splits = jax.random.split(jax.random.key(seed), 8)
    own_keys = jax.random.split(jax.random.fold_in(splits[7], part), 8)
    tokens = scatter_about(own_keys[0], (TOKENS, D), 1.0, 6.0, ((0, 4), (1, 4)))
    grad_out = scatter_about(own_keys[1], (TOKENS, D), 0.1, 0.59765625, ((0, 4), (1, 4)))
    expert_ids_keys = jax.random.split(jax.random.fold_in(own_keys[2], 1), TOKENS // TOK_DEV)
    expert_ids_turns = jax.random.permutation(jax.random.fold_in(own_keys[2], 3), TOKENS // TOK_DEV)
    expert_ids = jax.vmap(lambda own, number: shared_out(jax.random.fold_in(own_keys[2], 2), own, number, TOK_DEV, EXPERTS, TOP, CAP, 1))(expert_ids_keys, expert_ids_turns).reshape((TOKENS, TOP))
    route_probs = jnp.clip(0.1 + 0.9 * jax.random.uniform(own_keys[3], (TOKENS, TOP), jnp.float32) ** level_of(own_keys[3], (TOKENS, TOP), ((0, 4),), -0.2, 0.2), 0.1, 1.0)
    gate_w = scatter_about(splits[4], (EXPERTS, D, FF), D ** -0.5, 0.09375, ((0, 4), (2, 4)))
    up_w = scatter_about(splits[5], (EXPERTS, D, FF), D ** -0.5, 0.09375, ((0, 4), (2, 4)))
    down_w = scatter_about(splits[6], (EXPERTS, FF, D), FF ** -0.5, 0.15625, ((0, 4), (1, 4)))
    return {"tokens": tokens, "grad_out": grad_out, "expert_ids": expert_ids, "route_probs": route_probs, "gate_w": gate_w, "up_w": up_w, "down_w": down_w}


def rounded(value):
    return lax.optimization_barrier(value.astype(jnp.bfloat16))


def route_tables(routed, weights):
    flat_ids = routed.reshape(-1).astype(jnp.int32)
    onehot = (flat_ids[:, None] == jnp.arange(EXPERTS, dtype=jnp.int32)[None, :]).astype(jnp.int32)
    earlier = jnp.cumsum(onehot, axis=0) - onehot
    slot_index = jnp.sum(earlier * onehot, axis=1).astype(jnp.int32)
    target = (flat_ids * CAP + slot_index).astype(jnp.int32)
    cells = jnp.arange(EXPERTS * CAP, dtype=jnp.int32)
    match = cells[:, None] == target[None, :]
    owner = jnp.arange(flat_ids.shape[0], dtype=jnp.int32) // TOP
    filled = jnp.any(match, axis=1)
    token_of = jnp.sum(jnp.where(match, owner[None, :], 0), axis=1).astype(jnp.int32)
    weight_of = jnp.sum(jnp.where(match, weights.reshape(-1)[None, :], 0.0), axis=1)
    return target, token_of, weight_of, filled


def place_rows(features, grads, token_of, weight_of, filled):
    width = features.shape[1]
    slot_x = jnp.where(filled[:, None], jnp.take(features, token_of, axis=0), 0).astype(jnp.bfloat16)
    scaled = weight_of[:, None] * jnp.take(grads, token_of, axis=0).astype(jnp.float32)
    slot_g = rounded(jnp.where(filled[:, None], scaled, 0.0))
    return slot_x.reshape(EXPERTS, CAP, width), slot_g.reshape(EXPERTS, CAP, width)


def one_expert(bundle):
    slot_x, slot_g, w_gate, w_up, w_down = bundle
    many = slot_x.shape[0]
    width = FF // N_HID
    float_x = slot_x.astype(jnp.float32)
    float_g = slot_g.astype(jnp.float32)
    gate_f = w_gate.astype(jnp.float32)
    up_f = w_up.astype(jnp.float32)
    gate_value = jnp.dot(float_x, gate_f)
    up_value = jnp.dot(float_x, up_f)
    sigmoid_gate = jax.nn.sigmoid(gate_value)
    activated = gate_value * sigmoid_gate
    hidden = rounded(activated * up_value)
    grad_down = jnp.dot(hidden.astype(jnp.float32).T, float_g).astype(jnp.bfloat16)
    d_hidden = jnp.dot(float_g, w_down.astype(jnp.float32).T)
    d_gate_h = rounded(d_hidden * up_value * sigmoid_gate * (1.0 + gate_value * (1.0 - sigmoid_gate)))
    d_up_h = rounded(d_hidden * activated)
    grad_gate = jnp.dot(float_x.T, d_gate_h.astype(jnp.float32)).astype(jnp.bfloat16)
    grad_up = jnp.dot(float_x.T, d_up_h.astype(jnp.float32)).astype(jnp.bfloat16)
    gate_parts = d_gate_h.astype(jnp.float32).reshape(many, N_HID, width).transpose(1, 0, 2)
    up_parts = d_up_h.astype(jnp.float32).reshape(many, N_HID, width).transpose(1, 0, 2)
    wgate_parts = gate_f.reshape(D, N_HID, width).transpose(1, 0, 2)
    wup_parts = up_f.reshape(D, N_HID, width).transpose(1, 0, 2)

    def add_part(total, piece):
        part_gate, part_up, part_wgate, part_wup = piece
        term = jnp.dot(part_gate, part_wgate.T) + jnp.dot(part_up, part_wup.T)
        return total + rounded(term).astype(jnp.float32), None

    start = jnp.zeros((many, D), jnp.float32)
    total, _ = lax.scan(add_part, start, (gate_parts, up_parts, wgate_parts, wup_parts))
    return grad_gate, grad_up, grad_down, total.astype(jnp.bfloat16)


def reference(tokens, grad_out, expert_ids, route_probs, gate_w, up_w, down_w):
    routed = expert_ids.reshape(N_BLK, TOK_DEV, TOP)
    weights = route_probs.reshape(N_BLK, TOK_DEV, TOP)
    target, token_of, weight_of, filled = jax.vmap(route_tables)(routed, weights)
    group_x = tokens.reshape(N_BLK, TOK_DEV, D)
    group_g = grad_out.reshape(N_BLK, TOK_DEV, D)
    slot_x, slot_g = jax.vmap(place_rows)(group_x, group_g, token_of, weight_of, filled)
    rows_x = jnp.transpose(slot_x, (1, 0, 2, 3)).reshape(EXPERTS, N_BLK * CAP, D)
    rows_g = jnp.transpose(slot_g, (1, 0, 2, 3)).reshape(EXPERTS, N_BLK * CAP, D)
    grad_gate, grad_up, grad_down, slot_dx = lax.map(one_expert, (rows_x, rows_g, gate_w, up_w, down_w))
    returned = slot_dx.reshape(EXPERTS, N_BLK, CAP, D).transpose(1, 0, 2, 3).reshape(N_BLK, EXPERTS * CAP, D)

    def collect(group_rows, group_target):
        picked = jnp.take(group_rows, group_target, axis=0).astype(jnp.float32)
        return jnp.sum(picked.reshape(TOK_DEV, TOP, D), axis=1)

    grad_tokens = jax.vmap(collect)(returned, target).reshape(TOKENS, D).astype(jnp.bfloat16)
    return grad_tokens, grad_gate, grad_up, grad_down
```

```python
import functools
import jax
import jax.numpy as jnp
from jax import lax
from jax.experimental import pallas as pl
from jax.experimental.pallas import tpu as pltpu
from jax.sharding import PartitionSpec as P

TOP = 8
EXPERTS = 16
CAP = 68


def route_tables(routed, weights):
    flat_ids = routed.reshape(-1)
    onehot = (flat_ids[:, None] == jnp.arange(EXPERTS, dtype=jnp.int32)[None, :]).astype(jnp.int32)
    earlier = jnp.cumsum(onehot, axis=0) - onehot
    slot_index = jnp.sum(earlier * onehot, axis=1)
    target = flat_ids * CAP + slot_index
    cells = jnp.arange(EXPERTS * CAP, dtype=jnp.int32)
    match = cells[:, None] == target[None, :]
    owner = jnp.arange(flat_ids.shape[0], dtype=jnp.int32) // TOP
    filled = jnp.any(match, axis=1)
    token_of = jnp.sum(jnp.where(match, owner[None, :], 0), axis=1)
    weight_of = jnp.sum(jnp.where(match, weights.reshape(-1)[None, :], 0.0), axis=1)
    return (target, token_of, weight_of, filled)


def place_rows(features, grads, token_of, weight_of, filled):
    width = features.shape[1]
    slot_x = jnp.where(filled[:, None], jnp.take(features, token_of, axis=0), 0)
    scaled = weight_of[:, None] * jnp.take(grads, token_of, axis=0).astype(jnp.float32)
    slot_g = jnp.where(filled[:, None], scaled, 0.0).astype(jnp.bfloat16)
    return (slot_x.reshape(EXPERTS, CAP, width), slot_g.reshape(EXPERTS, CAP, width))


def by_slots(tokens, grad_out, expert_ids, route_probs, gate_w, up_w, down_w):
    local_tokens = tokens.shape[0]
    hidden_part = gate_w.shape[2]
    target, token_of, weight_of, filled = route_tables(expert_ids, route_probs)
    whole_x, whole_g = (
        lax.all_gather(tokens, "hid", axis=1, tiled=True),
        lax.all_gather(grad_out, "hid", axis=1, tiled=True),
    )
    send_x, send_g = place_rows(whole_x, whole_g, token_of, weight_of, filled)
    recv_x, recv_g = (
        lax.all_to_all(send_x, "blk", split_axis=0, concat_axis=1, tiled=True),
        lax.all_to_all(send_g, "blk", split_axis=0, concat_axis=1, tiled=True),
    )
    both_weights = jnp.concatenate((gate_w, up_w), axis=2)
    both_values = jnp.einsum(
        "erd,edf->erf", recv_x, both_weights, preferred_element_type=jnp.float32
    )
    gate_value = both_values[:, :, :hidden_part]
    up_value = both_values[:, :, hidden_part:]
    sigmoid_gate = jax.nn.sigmoid(gate_value)
    activated = gate_value * sigmoid_gate
    hidden = (activated * up_value).astype(jnp.bfloat16)
    grad_down = jnp.einsum(
        "erf,erd->efd", hidden, recv_g, preferred_element_type=jnp.float32
    ).astype(jnp.bfloat16)
    d_hidden = jnp.einsum("erd,efd->erf", recv_g, down_w, preferred_element_type=jnp.float32)
    d_gate_h = (
        d_hidden * up_value * sigmoid_gate * (1.0 + gate_value * (1.0 - sigmoid_gate))
    ).astype(jnp.bfloat16)
    d_up_h = (d_hidden * activated).astype(jnp.bfloat16)
    both_grads = jnp.concatenate((d_gate_h, d_up_h), axis=2)
    weight_grads = jnp.einsum(
        "erd,erf->edf", recv_x, both_grads, preferred_element_type=jnp.float32
    ).astype(jnp.bfloat16)
    grad_gate = weight_grads[:, :, :hidden_part]
    grad_up = weight_grads[:, :, hidden_part:]
    summed = lax.psum_scatter(
        jnp.einsum(
            "edf,erf->der", both_weights, both_grads, preferred_element_type=jnp.float32
        ).astype(jnp.bfloat16),
        "hid",
        scatter_dimension=0,
        tiled=True,
    ).astype(jnp.float32)
    shared = jnp.transpose(summed, (1, 2, 0)).astype(jnp.bfloat16)
    returned = lax.all_to_all(shared, "blk", split_axis=1, concat_axis=0, tiled=True)
    flat_back = returned.reshape(EXPERTS * CAP, returned.shape[2]).astype(jnp.float32)
    picked = jnp.take(flat_back, target, axis=0).reshape(local_tokens, TOP, returned.shape[2])
    grad_tokens = jnp.sum(picked, axis=1).astype(jnp.bfloat16)
    return (grad_tokens, grad_gate, grad_up, grad_down)

TILE = 1024
VMEM_ROOM = 60 * 1024 * 1024
ROWS_ROWS = (((0,), (0,)), ((), ()))
COLS_COLS = (((1,), (1,)), ((), ()))


def matmul(a, b, dims=(((1,), (0,)), ((), ()))):
    return lax.dot_general(a, b, dims, preferred_element_type=jnp.float32)


def expert_kernel(
    half, x_ref, g_ref, slot_ref, prob_ref, gate_ref, up_ref, down_ref,
    dx_ref, ggate_ref, gup_ref, gdown_ref,
    rows_x, rows_g, gate_sum, up_sum, dh_sum, token_dx, out_gate, out_up, out_down, sems,
):
    expert = pl.program_id(0)
    last = pl.num_programs(0) - 1
    width = x_ref.shape[1]
    many = x_ref.shape[0]
    depth = many // 2
    hidden_part = gate_ref.shape[2]

    def copies(index):
        return (
            pltpu.make_async_copy(out_down, gdown_ref.at[index], sems.at[0]),
            pltpu.make_async_copy(out_gate, ggate_ref.at[index], sems.at[1]),
            pltpu.make_async_copy(out_up, gup_ref.at[index], sems.at[2]),
        )

    slots = slot_ref[0]
    probs = prob_ref[0]
    places = []
    weights = []
    for part in range(2):
        match = slots[:, part * depth:(part + 1) * depth] == lax.broadcasted_iota(
            jnp.int32, (half, depth), 0
        )
        weights.append(
            jnp.sum(jnp.where(match, probs[:, part * depth:(part + 1) * depth], 0.0), axis=1, keepdims=True)
        )
        places.append(jnp.where(match, 1.0, 0.0).astype(jnp.bfloat16))
    weight = jnp.concatenate(weights, axis=0)

    gate_sum[...] = jnp.zeros_like(gate_sum)
    up_sum[...] = jnp.zeros_like(up_sum)
    dh_sum[...] = jnp.zeros_like(dh_sum)

    @pl.loop(0, width // TILE)
    def _(step):
        cols = pl.ds(pl.multiple_of(step * TILE, TILE), TILE)
        x_tile = jnp.concatenate(
            [matmul(places[p], x_ref[p * depth:(p + 1) * depth, cols]) for p in range(2)], axis=0
        ).astype(jnp.bfloat16)
        g_tile = (
            weight
            * jnp.concatenate(
                [matmul(places[p], g_ref[p * depth:(p + 1) * depth, cols]) for p in range(2)], axis=0
            )
        ).astype(jnp.bfloat16)
        rows_x[:, cols] = x_tile
        rows_g[:, cols] = g_tile
        gate_sum[...] += matmul(x_tile, gate_ref[0, cols, :])
        up_sum[...] += matmul(x_tile, up_ref[0, cols, :])
        dh_sum[...] += matmul(g_tile, down_ref[0, :, cols], COLS_COLS)

    gate_value = gate_sum[...]
    up_value = up_sum[...]
    d_hidden = dh_sum[...]
    sigmoid_gate = jax.nn.sigmoid(gate_value)
    activated = gate_value * sigmoid_gate
    hidden = (activated * up_value).astype(jnp.bfloat16)
    d_gate_h = (
        d_hidden * up_value * sigmoid_gate * (1.0 + gate_value * (1.0 - sigmoid_gate))
    ).astype(jnp.bfloat16)
    d_up_h = (d_hidden * activated).astype(jnp.bfloat16)
    d_both = jnp.concatenate((d_gate_h, d_up_h), axis=1)

    @pl.when(expert > 0)
    def _():
        for copy in copies(expert - 1):
            copy.wait()

    @pl.loop(0, width // TILE)
    def _(step):
        cols = pl.ds(pl.multiple_of(step * TILE, TILE), TILE)
        out_down[:, cols] = matmul(hidden, rows_g[:, cols], ROWS_ROWS).astype(jnp.bfloat16)
        both = matmul(rows_x[:, cols], d_both, ROWS_ROWS).astype(jnp.bfloat16)
        out_gate[cols, :] = both[:, :hidden_part]
        out_up[cols, :] = both[:, hidden_part:]
        slot_dx = matmul(d_gate_h, gate_ref[0, cols, :], COLS_COLS) + matmul(
            d_up_h, up_ref[0, cols, :], COLS_COLS
        )
        for p in range(2):
            term = matmul(
                places[p], slot_dx[p * half:(p + 1) * half].astype(jnp.bfloat16), ROWS_ROWS
            )
            area = (slice(p * depth, (p + 1) * depth), cols)

            @pl.when(expert == 0)
            def _():
                token_dx[area] = term

            @pl.when((expert > 0) & (expert < last))
            def _():
                token_dx[area] += term

            @pl.when((expert > 0) & (expert == last))
            def _():
                dx_ref[area] = (token_dx[area] + term).astype(jnp.bfloat16)

    for copy in copies(expert):
        copy.start()

    @pl.when(expert == last)
    def _():
        for copy in copies(expert):
            copy.wait()


def expert_pass(all_x, all_g, slots, probs, gate_w, up_w, down_w, half):
    experts, width, hidden_part = gate_w.shape
    many = all_x.shape[0]
    rows = 2 * half
    whole = pl.BlockSpec((many, width), lambda e: (0, 0), pipeline_mode=pl.Buffered(1))
    line = pl.BlockSpec((1, 1, many), lambda e: (e, 0, 0))
    weight_in = pl.BlockSpec((1, width, hidden_part), lambda e: (e, 0, 0))
    weight_out = pl.BlockSpec((1, hidden_part, width), lambda e: (e, 0, 0))
    bf16 = jnp.bfloat16
    return pl.pallas_call(
        functools.partial(expert_kernel, half),
        grid=(experts,),
        in_specs=[whole, whole, line, line, weight_in, weight_in, weight_out],
        out_specs=[
            pl.BlockSpec((many, width), lambda e: (0, 0)),
            pl.BlockSpec(memory_space=pl.ANY),
            pl.BlockSpec(memory_space=pl.ANY),
            pl.BlockSpec(memory_space=pl.ANY),
        ],
        out_shape=[
            jax.ShapeDtypeStruct((many, width), bf16),
            jax.ShapeDtypeStruct(gate_w.shape, bf16),
            jax.ShapeDtypeStruct(up_w.shape, bf16),
            jax.ShapeDtypeStruct(down_w.shape, bf16),
        ],
        scratch_shapes=[
            pltpu.VMEM((rows, width), bf16),
            pltpu.VMEM((rows, width), bf16),
            pltpu.VMEM((rows, hidden_part), jnp.float32),
            pltpu.VMEM((rows, hidden_part), jnp.float32),
            pltpu.VMEM((rows, hidden_part), jnp.float32),
            pltpu.VMEM((many, width), jnp.float32),
            pltpu.VMEM((width, hidden_part), bf16),
            pltpu.VMEM((width, hidden_part), bf16),
            pltpu.VMEM((hidden_part, width), bf16),
            pltpu.SemaphoreType.DMA((3,)),
        ],
        compiler_params=pltpu.CompilerParams(
            dimension_semantics=("arbitrary",), vmem_limit_bytes=VMEM_ROOM
        ),
        cost_estimate=pl.CostEstimate(
            flops=16 * experts * rows * width * hidden_part,
            bytes_accessed=12 * experts * width * hidden_part,
            transcendentals=experts * rows * hidden_part,
        ),
    )(all_x, all_g, slots, probs, gate_w, up_w, down_w)


def local_routes(expert_ids, route_probs, experts, depth):
    ids = lax.all_gather(expert_ids, "blk", axis=0, tiled=True)
    probs = lax.all_gather(route_probs, "blk", axis=0, tiled=True)
    first = lax.axis_index("blk") * experts
    mine = first + jnp.arange(experts, dtype=jnp.int32)
    same = ids[None, :, :] == mine[:, None, None]
    member = jnp.any(same, axis=2)
    prob = jnp.sum(jnp.where(same, probs[None], 0.0), axis=2)
    many = ids.shape[0]
    halves = member.astype(jnp.int32).reshape(experts, many // depth, depth)
    earlier = (jnp.cumsum(halves, axis=2) - halves).reshape(experts, many)
    slot = jnp.where(member, earlier, -1)
    return slot.reshape(experts, 1, many), prob.reshape(experts, 1, many)


def by_tokens(tokens, grad_out, expert_ids, route_probs, gate_w, up_w, down_w):
    experts = gate_w.shape[0]
    n_blk = lax.axis_size("blk")
    depth = n_blk * tokens.shape[0] // 2
    half = n_blk * CAP // 2
    slots, probs = local_routes(expert_ids, route_probs, experts, depth)
    all_x, all_g = (
        lax.all_gather(
            lax.all_gather(part, "hid", axis=1, tiled=True), "blk", axis=0, tiled=True
        )
        for part in (tokens, grad_out)
    )
    dx, grad_gate, grad_up, grad_down = expert_pass(
        all_x, all_g, slots, probs, gate_w, up_w, down_w, half
    )
    dx = lax.psum_scatter(dx, "blk", scatter_dimension=0, tiled=True)
    grad_tokens = lax.psum_scatter(dx, "hid", scatter_dimension=1, tiled=True)
    return (grad_tokens, grad_gate, grad_up, grad_down)


def fits(many, width, hidden_part, experts, n_blk):
    rows = n_blk * CAP
    held = 2 * (2 * 3 + 3) * width * hidden_part + (2 * 2 + 2 * 2 + 4) * many * width
    held += 4 * rows * width + 12 * rows * hidden_part
    aligned = hidden_part % 128 == 0 and width % TILE == 0 and n_blk % 4 == 0
    return aligned and experts > 1 and (many // 2) % 128 == 0 and held < VMEM_ROOM


def per_device(tokens, grad_out, expert_ids, route_probs, gate_w, up_w, down_w):
    n_blk = lax.axis_size("blk")
    experts, width, hidden_part = gate_w.shape
    plan = by_tokens if fits(n_blk * tokens.shape[0], width, hidden_part, experts, n_blk) else by_slots
    return plan(tokens, grad_out, expert_ids, route_probs, gate_w, up_w, down_w)


def solution(mesh):
    placed = (
        P(("grp", "blk"), "hid"),
        P(("grp", "blk"), "hid"),
        P(("grp", "blk"), None),
        P(("grp", "blk"), None),
        P("blk", None, "hid"),
        P("blk", None, "hid"),
        P("blk", "hid", None),
    )
    return jax.shard_map(
        per_device,
        mesh=mesh,
        in_specs=placed,
        out_specs=(
            P(("grp", "blk"), "hid"),
            P(("grp", "blk"), None, "hid"),
            P(("grp", "blk"), None, "hid"),
            P(("grp", "blk"), "hid", None),
        ),
        check_vma=False,
    )
```

```python
import functools
import jax
import jax.numpy as jnp
from jax import lax
from jax.experimental import pallas as pl
from jax.experimental.pallas import tpu as pltpu
from jax.sharding import PartitionSpec as P

TOP = 8
EXPERTS = 16
CAP = 68


def route_tables(routed, weights):
    flat_ids = routed.reshape(-1)
    onehot = (flat_ids[:, None] == jnp.arange(EXPERTS, dtype=jnp.int32)[None, :]).astype(jnp.int32)
    earlier = jnp.cumsum(onehot, axis=0) - onehot
    slot_index = jnp.sum(earlier * onehot, axis=1)
    target = flat_ids * CAP + slot_index
    cells = jnp.arange(EXPERTS * CAP, dtype=jnp.int32)
    match = cells[:, None] == target[None, :]
    owner = jnp.arange(flat_ids.shape[0], dtype=jnp.int32) // TOP
    filled = jnp.any(match, axis=1)
    token_of = jnp.sum(jnp.where(match, owner[None, :], 0), axis=1)
    weight_of = jnp.sum(jnp.where(match, weights.reshape(-1)[None, :], 0.0), axis=1)
    return (target, token_of, weight_of, filled)


def place_rows(features, grads, token_of, weight_of, filled):
    width = features.shape[1]
    slot_x = jnp.where(filled[:, None], jnp.take(features, token_of, axis=0), 0)
    scaled = weight_of[:, None] * jnp.take(grads, token_of, axis=0).astype(jnp.float32)
    slot_g = jnp.where(filled[:, None], scaled, 0.0).astype(jnp.bfloat16)
    return (slot_x.reshape(EXPERTS, CAP, width), slot_g.reshape(EXPERTS, CAP, width))


def by_slots(tokens, grad_out, expert_ids, route_probs, gate_w, up_w, down_w):
    local_tokens = tokens.shape[0]
    hidden_part = gate_w.shape[2]
    target, token_of, weight_of, filled = route_tables(expert_ids, route_probs)
    whole_x, whole_g = (
        lax.all_gather(tokens, "hid", axis=1, tiled=True),
        lax.all_gather(grad_out, "hid", axis=1, tiled=True),
    )
    send_x, send_g = place_rows(whole_x, whole_g, token_of, weight_of, filled)
    recv_x, recv_g = (
        lax.all_to_all(send_x, "blk", split_axis=0, concat_axis=1, tiled=True),
        lax.all_to_all(send_g, "blk", split_axis=0, concat_axis=1, tiled=True),
    )
    both_weights = jnp.concatenate((gate_w, up_w), axis=2)
    both_values = jnp.einsum(
        "erd,edf->erf", recv_x, both_weights, preferred_element_type=jnp.float32
    )
    gate_value = both_values[:, :, :hidden_part]
    up_value = both_values[:, :, hidden_part:]
    sigmoid_gate = jax.nn.sigmoid(gate_value)
    activated = gate_value * sigmoid_gate
    hidden = (activated * up_value).astype(jnp.bfloat16)
    grad_down = jnp.einsum(
        "erf,erd->efd", hidden, recv_g, preferred_element_type=jnp.float32
    ).astype(jnp.bfloat16)
    d_hidden = jnp.einsum("erd,efd->erf", recv_g, down_w, preferred_element_type=jnp.float32)
    d_gate_h = (
        d_hidden * up_value * sigmoid_gate * (1.0 + gate_value * (1.0 - sigmoid_gate))
    ).astype(jnp.bfloat16)
    d_up_h = (d_hidden * activated).astype(jnp.bfloat16)
    both_grads = jnp.concatenate((d_gate_h, d_up_h), axis=2)
    weight_grads = jnp.einsum(
        "erd,erf->edf", recv_x, both_grads, preferred_element_type=jnp.float32
    ).astype(jnp.bfloat16)
    grad_gate = weight_grads[:, :, :hidden_part]
    grad_up = weight_grads[:, :, hidden_part:]
    summed = lax.psum_scatter(
        jnp.einsum(
            "edf,erf->der", both_weights, both_grads, preferred_element_type=jnp.float32
        ).astype(jnp.bfloat16),
        "hid",
        scatter_dimension=0,
        tiled=True,
    ).astype(jnp.float32)
    shared = jnp.transpose(summed, (1, 2, 0)).astype(jnp.bfloat16)
    returned = lax.all_to_all(shared, "blk", split_axis=1, concat_axis=0, tiled=True)
    flat_back = returned.reshape(EXPERTS * CAP, returned.shape[2]).astype(jnp.float32)
    picked = jnp.take(flat_back, target, axis=0).reshape(local_tokens, TOP, returned.shape[2])
    grad_tokens = jnp.sum(picked, axis=1).astype(jnp.bfloat16)
    return (grad_tokens, grad_gate, grad_up, grad_down)

TILE = 1024
MESH = pl.DeviceIdType.MESH
VMEM_ROOM = 60 * 1024 * 1024
ROWS_ROWS = (((0,), (0,)), ((), ()))
COLS_COLS = (((1,), (1,)), ((), ()))


def matmul(a, b, dims=(((1,), (0,)), ((), ()))):
    return lax.dot_general(a, b, dims, preferred_element_type=jnp.float32)


def expert_kernel(
    half, x_ref, g_ref, slot_ref, prob_ref, gate_ref, up_ref, down_ref,
    dx_ref, ggate_ref, gup_ref, gdown_ref,
    rows_x, rows_g, both_sum, dh_sum, token_dx, out_gate, out_up, out_down, sems,
):
    expert = pl.program_id(0)
    last = pl.num_programs(0) - 1
    width = x_ref.shape[1]
    many = x_ref.shape[0]
    depth = many // 2
    hidden_part = gate_ref.shape[2]

    def copies(index):
        return (
            pltpu.make_async_copy(out_down, gdown_ref.at[index], sems.at[0]),
            pltpu.make_async_copy(out_gate, ggate_ref.at[index], sems.at[1]),
            pltpu.make_async_copy(out_up, gup_ref.at[index], sems.at[2]),
        )

    slots = slot_ref[0]
    probs = prob_ref[0]
    places = []
    weights = []
    for part in range(2):
        match = slots[:, part * depth:(part + 1) * depth] == lax.broadcasted_iota(
            jnp.int32, (half, depth), 0
        )
        weights.append(
            jnp.sum(jnp.where(match, probs[:, part * depth:(part + 1) * depth], 0.0), axis=1, keepdims=True)
        )
        places.append(jnp.where(match, 1.0, 0.0).astype(jnp.bfloat16))
    weight = jnp.concatenate(weights, axis=0)

    both_sum[...] = jnp.zeros_like(both_sum)
    dh_sum[...] = jnp.zeros_like(dh_sum)

    @pl.loop(0, width // TILE)
    def _(step):
        cols = pl.ds(pl.multiple_of(step * TILE, TILE), TILE)
        x_tile = jnp.concatenate(
            [matmul(places[p], x_ref[p * depth:(p + 1) * depth, cols]) for p in range(2)], axis=0
        ).astype(jnp.bfloat16)
        g_tile = (
            weight
            * jnp.concatenate(
                [matmul(places[p], g_ref[p * depth:(p + 1) * depth, cols]) for p in range(2)], axis=0
            )
        ).astype(jnp.bfloat16)
        rows_x[:, cols] = x_tile
        rows_g[:, cols] = g_tile
        both_w = jnp.concatenate((gate_ref[0, cols, :], up_ref[0, cols, :]), axis=1)
        both_sum[...] += matmul(x_tile, both_w)
        dh_sum[...] += matmul(g_tile, down_ref[0, :, cols], COLS_COLS)

    gate_value = both_sum[:, :hidden_part]
    up_value = both_sum[:, hidden_part:]
    d_hidden = dh_sum[...]
    sigmoid_gate = jax.nn.sigmoid(gate_value)
    activated = gate_value * sigmoid_gate
    hidden = (activated * up_value).astype(jnp.bfloat16)
    d_gate_h = (
        d_hidden * up_value * sigmoid_gate * (1.0 + gate_value * (1.0 - sigmoid_gate))
    ).astype(jnp.bfloat16)
    d_up_h = (d_hidden * activated).astype(jnp.bfloat16)
    d_both = jnp.concatenate((d_gate_h, d_up_h), axis=1)

    @pl.when(expert > 0)
    def _():
        for copy in copies(expert - 1):
            copy.wait()

    @pl.loop(0, width // TILE)
    def _(step):
        cols = pl.ds(pl.multiple_of(step * TILE, TILE), TILE)
        out_down[:, cols] = matmul(hidden, rows_g[:, cols], ROWS_ROWS).astype(jnp.bfloat16)
        both = matmul(rows_x[:, cols], d_both, ROWS_ROWS).astype(jnp.bfloat16)
        out_gate[cols, :] = both[:, :hidden_part]
        out_up[cols, :] = both[:, hidden_part:]
        both_w = jnp.concatenate((gate_ref[0, cols, :], up_ref[0, cols, :]), axis=1)
        slot_dx = matmul(d_both, both_w, COLS_COLS)
        for p in range(2):
            term = matmul(
                places[p], slot_dx[p * half:(p + 1) * half].astype(jnp.bfloat16), ROWS_ROWS
            )
            area = (slice(p * depth, (p + 1) * depth), cols)

            @pl.when(expert == 0)
            def _():
                token_dx[area] = term

            @pl.when((expert > 0) & (expert < last))
            def _():
                token_dx[area] += term

            @pl.when((expert > 0) & (expert == last))
            def _():
                dx_ref[area] = (token_dx[area] + term).astype(jnp.bfloat16)

    for copy in copies(expert):
        copy.start()

    @pl.when(expert == last)
    def _():
        for copy in copies(expert):
            copy.wait()


def expert_pass(all_x, all_g, slots, probs, gate_w, up_w, down_w, half):
    experts, width, hidden_part = gate_w.shape
    many = all_x.shape[0]
    rows = 2 * half
    whole = pl.BlockSpec((many, width), lambda e: (0, 0), pipeline_mode=pl.Buffered(1))
    line = pl.BlockSpec((1, 1, many), lambda e: (e, 0, 0))
    weight_in = pl.BlockSpec((1, width, hidden_part), lambda e: (e, 0, 0))
    weight_out = pl.BlockSpec((1, hidden_part, width), lambda e: (e, 0, 0))
    bf16 = jnp.bfloat16
    return pl.pallas_call(
        functools.partial(expert_kernel, half),
        grid=(experts,),
        in_specs=[whole, whole, line, line, weight_in, weight_in, weight_out],
        out_specs=[
            pl.BlockSpec((many, width), lambda e: (0, 0)),
            pl.BlockSpec(memory_space=pl.ANY),
            pl.BlockSpec(memory_space=pl.ANY),
            pl.BlockSpec(memory_space=pl.ANY),
        ],
        out_shape=[
            jax.ShapeDtypeStruct((many, width), bf16),
            jax.ShapeDtypeStruct(gate_w.shape, bf16),
            jax.ShapeDtypeStruct(up_w.shape, bf16),
            jax.ShapeDtypeStruct(down_w.shape, bf16),
        ],
        scratch_shapes=[
            pltpu.VMEM((rows, width), bf16),
            pltpu.VMEM((rows, width), bf16),
            pltpu.VMEM((rows, 2 * hidden_part), jnp.float32),
            pltpu.VMEM((rows, hidden_part), jnp.float32),
            pltpu.VMEM((many, width), jnp.float32),
            pltpu.VMEM((width, hidden_part), bf16),
            pltpu.VMEM((width, hidden_part), bf16),
            pltpu.VMEM((hidden_part, width), bf16),
            pltpu.SemaphoreType.DMA((3,)),
        ],
        compiler_params=pltpu.CompilerParams(
            dimension_semantics=("arbitrary",), vmem_limit_bytes=VMEM_ROOM
        ),
        cost_estimate=pl.CostEstimate(
            flops=16 * experts * rows * width * hidden_part,
            bytes_accessed=12 * experts * width * hidden_part,
            transcendentals=experts * rows * hidden_part,
        ),
    )(all_x, all_g, slots, probs, gate_w, up_w, down_w)


def greet(blk, hid, n_hid):
    barrier = pltpu.get_barrier_semaphore()
    for hop in range(1, 4):
        pl.semaphore_signal(
            barrier, inc=1, device_id={"blk": lax.rem(blk + hop, 4)}, device_id_type=MESH
        )

    @pl.when(hid > 0)
    def _():
        pl.semaphore_signal(barrier, inc=1, device_id={"hid": hid - 1}, device_id_type=MESH)

    @pl.when(hid < n_hid - 1)
    def _():
        pl.semaphore_signal(barrier, inc=1, device_id={"hid": hid + 1}, device_id_type=MESH)

    below = lax.div(hid + n_hid - 1, n_hid)
    above = lax.div(2 * n_hid - 2 - hid, n_hid)
    pl.semaphore_wait(barrier, 3 + below + above)


def gather_kernel(
    n_hid, x_ref, g_ref, ids_ref, prob_ref, all_x, all_g, all_ids, all_prob,
    own_sems, line_send, x_send, core_send, recv, small_send, small_recv,
):
    blk = lax.axis_index("blk")
    hid = lax.axis_index("hid")
    rows, part = x_ref.shape
    sibling = blk + 1 - 2 * lax.rem(blk, 2)
    across = lax.rem(blk + 2, 4)
    sources = (x_ref, g_ref)
    fulls = (all_x, all_g)
    smalls = ((ids_ref, all_ids), (prob_ref, all_prob))

    def area(which, owner, column):
        return fulls[which].at[
            pl.ds(pl.multiple_of(owner * rows, rows), rows),
            pl.ds(pl.multiple_of(column * part, part), part),
        ]

    def small_area(which, owner):
        return smalls[which][1].at[pl.ds(pl.multiple_of(owner * TOP, TOP), TOP), :]

    def push(which, owner, column, sem, device, own=False):
        return pltpu.make_async_remote_copy(
            src_ref=sources[which] if own else area(which, owner, column),
            dst_ref=area(which, owner, column),
            send_sem=sem,
            recv_sem=recv.at[which, owner, column],
            device_id=device,
            device_id_type=MESH,
        )

    def up(which, column, own=False):
        return push(which, blk, column, line_send.at[0, which, column], {"hid": hid + 1}, own)

    def down(which, column, own=False):
        return push(which, blk, column, line_send.at[1, which, column], {"hid": hid - 1}, own)

    def line_sent(way, which, column):
        push(which, blk, column, line_send.at[way, which, column], {"blk": sibling}).wait_send()

    def over(which, column, own=False):
        return push(which, blk, column, x_send.at[which, column], {"blk": across}, own)

    def beside(which, index, column, own=False):
        owner = (blk, across)[index]
        return push(which, owner, column, core_send.at[index, which, column], {"blk": sibling}, own)

    def small(which, hop):
        return pltpu.make_async_remote_copy(
            src_ref=smalls[which][0],
            dst_ref=small_area(which, blk),
            send_sem=small_send.at[which, hop],
            recv_sem=small_recv.at[which, hop],
            device_id={"blk": lax.rem(blk + hop, 4)},
            device_id_type=MESH,
        )

    def landed(which, owner, column):
        push(which, owner, column, recv.at[which, owner, column], {"blk": sibling}).wait_recv()

    def keep():
        return [
            pltpu.make_async_copy(sources[w], area(w, blk, hid), own_sems.at[w]) for w in range(2)
        ] + [
            pltpu.make_async_copy(smalls[w][0], small_area(w, blk), own_sems.at[2 + w])
            for w in range(2)
        ]

    def from_across(step):
        for side in (-1, 1) if step else (1,):
            column = hid + side * step

            @pl.when((column >= 0) & (column < n_hid))
            def _():
                for which in range(2):
                    landed(which, across, column)
                    beside(which, 1, column).start()

    greet(blk, hid, n_hid)
    for which in range(2):
        @pl.when(hid < n_hid - 1)
        def _():
            up(which, hid, True).start()

        @pl.when(hid > 0)
        def _():
            down(which, hid, True).start()

        over(which, hid, True).start()
    for which in range(2):
        beside(which, 0, hid, True).start()
        for hop in range(1, 4):
            small(which, hop).start()
    for copy in keep():
        copy.start()
    for step in range(1, n_hid):
        @pl.when(hid - step >= 0)
        def _():
            column = hid - step
            for which in range(2):
                landed(which, blk, column)

                @pl.when(hid < n_hid - 1)
                def _():
                    up(which, column).start()

                over(which, column).start()
                beside(which, 0, column).start()

        @pl.when(hid + step < n_hid)
        def _():
            column = hid + step
            for which in range(2):
                landed(which, blk, column)

                @pl.when(hid > 0)
                def _():
                    down(which, column).start()

                over(which, column).start()
                beside(which, 0, column).start()

        from_across(step - 1)
    from_across(n_hid - 1)

    beyond = lax.rem(sibling + 2, 4)
    for column in range(n_hid):
        for which in range(2):
            landed(which, sibling, column)
            landed(which, beyond, column)
            over(which, column).wait_send()
            beside(which, 0, column).wait_send()
            beside(which, 1, column).wait_send()

            @pl.when((hid >= column) & (hid < n_hid - 1))
            def _():
                line_sent(0, which, column)

            @pl.when((hid <= column) & (hid > 0))
            def _():
                line_sent(1, which, column)

    for which in range(2):
        for hop in range(1, 4):
            small(which, hop).wait()
    for copy in keep():
        copy.wait()


def gather_all(tokens, grad_out, ids, probs, n_hid):
    rows, part = tokens.shape
    anywhere = pl.BlockSpec(memory_space=pl.ANY)
    full = jax.ShapeDtypeStruct((4 * rows, n_hid * part), tokens.dtype)
    dma = pltpu.SemaphoreType.DMA
    return pl.pallas_call(
        functools.partial(gather_kernel, n_hid),
        in_specs=[anywhere] * 4,
        out_specs=[anywhere] * 4,
        out_shape=[
            full,
            full,
            jax.ShapeDtypeStruct((4 * ids.shape[0], ids.shape[1]), ids.dtype),
            jax.ShapeDtypeStruct((4 * probs.shape[0], probs.shape[1]), probs.dtype),
        ],
        scratch_shapes=[
            dma((4,)),
            dma((2, 2, n_hid)),
            dma((2, n_hid)),
            dma((2, 2, n_hid)),
            dma((2, 4, n_hid)),
            dma((2, 4)),
            dma((2, 4)),
        ],
        compiler_params=pltpu.CompilerParams(collective_id=1, has_side_effects=True),
    )(tokens, grad_out, ids, probs)


def reduce_kernel(
    n_hid, dx_ref, out_ref, core_in, x_out, x_in, line_out, line_in,
    core_send, core_recv, x_send, x_recv, line_send, line_recv,
):
    blk = lax.axis_index("blk")
    hid = lax.axis_index("hid")
    rows, part = out_ref.shape
    sibling = blk + 1 - 2 * lax.rem(blk, 2)
    across = lax.rem(blk + 2, 4)
    beyond = lax.rem(sibling + 2, 4)

    def area(owner, column):
        return dx_ref.at[
            pl.ds(pl.multiple_of(owner * rows, rows), rows),
            pl.ds(pl.multiple_of(column * part, part), part),
        ]

    def wide(ref):
        return ref[...].astype(jnp.float32)

    def push(src, dst, send, recv, device):
        return pltpu.make_async_remote_copy(
            src_ref=src, dst_ref=dst, send_sem=send, recv_sem=recv,
            device_id=device, device_id_type=MESH,
        )

    def beside(index, column):
        return push(
            area((sibling, beyond)[index], column), core_in.at[index, column],
            core_send.at[index, column], core_recv.at[index, column], {"blk": sibling},
        )

    def over(column):
        return push(
            x_out.at[column], x_in.at[column], x_send.at[column], x_recv.at[column], {"blk": across}
        )

    def along(way, column):
        return push(
            line_out.at[column], line_in.at[way, column],
            line_send.at[column], line_recv.at[way, column], {"hid": hid + (1, -1)[way]},
        )

    def arrived(way, column):
        push(
            line_out.at[column], line_in.at[way, column],
            line_send.at[column], line_recv.at[way, column], {"blk": sibling},
        ).wait_recv()

    def line_sent(column):
        push(
            line_out.at[column], line_in.at[0, column],
            line_send.at[column], line_recv.at[0, column], {"blk": sibling},
        ).wait_send()

    def each(body):
        for step in range(n_hid - 1, 0, -1):
            for side in (1, -1):
                column = hid + side * step

                @pl.when((column >= 0) & (column < n_hid))
                def _():
                    body(column, side)

        body(hid, 0)

    def send_core(column, side):
        beside(1, column).start()
        beside(0, column).start()

    def send_x(column, side):
        beside(1, column).wait_recv()
        x_out[column] = (wide(area(across, column)) + wide(core_in.at[1, column])).astype(x_out.dtype)
        over(column).start()

    def send_line(column, side):
        beside(0, column).wait_recv()
        over(column).wait_recv()
        near = wide(area(blk, column)) + wide(core_in.at[0, column]) + wide(x_in.at[column])
        if side:
            way = 0 if side == 1 else 1
            inner = hid > 0 if side == 1 else hid < n_hid - 1

            @pl.when(inner)
            def _():
                arrived(way, column)
                line_out[column] = (near + wide(line_in.at[way, column])).astype(line_out.dtype)

            @pl.when(jnp.logical_not(inner))
            def _():
                line_out[column] = near.astype(line_out.dtype)

            along(way, column).start()
            return

        @pl.when(hid == 0)
        def _():
            arrived(1, column)
            out_ref[...] = (near + wide(line_in.at[1, column])).astype(out_ref.dtype)

        @pl.when(hid == n_hid - 1)
        def _():
            arrived(0, column)
            out_ref[...] = (near + wide(line_in.at[0, column])).astype(out_ref.dtype)

        @pl.when((hid > 0) & (hid < n_hid - 1))
        def _():
            arrived(0, column)
            arrived(1, column)
            out_ref[...] = (
                near + wide(line_in.at[0, column]) + wide(line_in.at[1, column])
            ).astype(out_ref.dtype)

    greet(blk, hid, n_hid)
    each(send_core)
    each(send_x)
    each(send_line)
    for column in range(n_hid):
        beside(0, column).wait_send()
        beside(1, column).wait_send()
        over(column).wait_send()

        @pl.when(hid != column)
        def _():
            line_sent(column)


def reduce_all(dx, rows, part, n_hid):
    bf16 = jnp.bfloat16
    dma = pltpu.SemaphoreType.DMA
    inside = pl.BlockSpec(memory_space=pltpu.VMEM)
    return pl.pallas_call(
        functools.partial(reduce_kernel, n_hid),
        in_specs=[inside],
        out_specs=inside,
        out_shape=jax.ShapeDtypeStruct((rows, part), bf16),
        scratch_shapes=[
            pltpu.VMEM((2, n_hid, rows, part), bf16),
            pltpu.VMEM((n_hid, rows, part), bf16),
            pltpu.VMEM((n_hid, rows, part), bf16),
            pltpu.VMEM((n_hid, rows, part), bf16),
            pltpu.VMEM((2, n_hid, rows, part), bf16),
            dma((2, n_hid)),
            dma((2, n_hid)),
            dma((n_hid,)),
            dma((n_hid,)),
            dma((n_hid,)),
            dma((2, n_hid)),
        ],
        compiler_params=pltpu.CompilerParams(
            collective_id=2, has_side_effects=True, vmem_limit_bytes=40 * 1024 * 1024
        ),
    )(dx)


def local_routes(ids, probs, experts, depth):
    first = lax.axis_index("blk") * experts
    mine = first + jnp.arange(experts, dtype=jnp.int32)
    groups = ids.shape[0] // TOP
    many = groups * ids.shape[1]
    same = ids.reshape(1, groups, TOP, -1) == mine[:, None, None, None]
    member = jnp.any(same, axis=2).reshape(experts, many)
    prob = jnp.sum(jnp.where(same, probs.reshape(1, groups, TOP, -1), 0.0), axis=2)
    before = jnp.arange(depth)[:, None] < jnp.arange(depth)[None, :]
    earlier = jnp.dot(
        member.reshape(-1, depth).astype(jnp.bfloat16),
        before.astype(jnp.bfloat16),
        preferred_element_type=jnp.float32,
    ).reshape(experts, many)
    slot = jnp.where(member, earlier.astype(jnp.int32), -1)
    return slot.reshape(experts, 1, many), prob.reshape(experts, 1, many)


def by_tokens(tokens, grad_out, expert_ids, route_probs, gate_w, up_w, down_w):
    experts = gate_w.shape[0]
    n_blk = lax.axis_size("blk")
    depth = n_blk * tokens.shape[0] // 2
    half = n_blk * CAP // 2
    n_hid = lax.axis_size("hid")
    all_x, all_g, ids, probs = gather_all(tokens, grad_out, expert_ids.T, route_probs.T, n_hid)
    slots, probs = local_routes(ids, probs, experts, depth)
    dx, grad_gate, grad_up, grad_down = expert_pass(
        all_x, all_g, slots, probs, gate_w, up_w, down_w, half
    )
    grad_tokens = reduce_all(dx, *tokens.shape, n_hid)
    return (grad_tokens, grad_gate, grad_up, grad_down)


def fits(many, width, hidden_part, experts, n_blk):
    rows = n_blk * CAP
    held = 2 * (2 * 3 + 3) * width * hidden_part + (2 * 2 + 2 * 2 + 4) * many * width
    held += 4 * rows * width + 12 * rows * hidden_part
    aligned = hidden_part % 128 == 0 and width % TILE == 0 and n_blk == 4
    return aligned and experts > 1 and (many // 2) % 128 == 0 and held < VMEM_ROOM


def per_device(tokens, grad_out, expert_ids, route_probs, gate_w, up_w, down_w):
    n_blk = lax.axis_size("blk")
    experts, width, hidden_part = gate_w.shape
    plan = by_tokens if fits(n_blk * tokens.shape[0], width, hidden_part, experts, n_blk) else by_slots
    return plan(tokens, grad_out, expert_ids, route_probs, gate_w, up_w, down_w)


def solution(mesh):
    placed = (
        P(("grp", "blk"), "hid"),
        P(("grp", "blk"), "hid"),
        P(("grp", "blk"), None),
        P(("grp", "blk"), None),
        P("blk", None, "hid"),
        P("blk", None, "hid"),
        P("blk", "hid", None),
    )
    return jax.shard_map(
        per_device,
        mesh=mesh,
        in_specs=placed,
        out_specs=(
            P(("grp", "blk"), "hid"),
            P(("grp", "blk"), None, "hid"),
            P(("grp", "blk"), None, "hid"),
            P(("grp", "blk"), "hid", None),
        ),
        check_vma=False,
    )
```
